32 devices in a mesh: rows: 8 (over z, y), cols: 4 (over x, core).
Axes of the slice: x: 2, y: 2, z: 4, core: 2. Of those that a mesh axis runs over, the one named last changes fastest.
Arguments:
- z_blocks: float32 [32, 4, 256, 256], P('rows', 'cols'), may hold values from -0.1875 to 0.1875
- z_cols: int32 [32, 4], P('rows', 'cols'), may hold values from 0 to 31, as said below
- z_count: int32 [32], P('rows'), may hold values from 1 to 4, as said below
- h_blocks: float32 [32, 4, 256, 256], P('rows', 'cols'), may hold values from -0.1875 to 0.1875
- h_cols: int32 [32, 4], P('rows', 'cols'), may hold values from 0 to 31, as said below
- h_count: int32 [32], P('rows'), may hold values from 1 to 4, as said below
- panel: float32 [32, 256, 64], P('rows'), may hold values from -6 to 6
Outputs:
- result: float32 [32, 256, 64], P('rows', 'cols')
The draws below stay inside these ranges and needn't reach their ends.
Inputs may be any that keep to these rules, and one draw needn't show every extreme that they name: `z_cols`: within a block row the column block indices of the slots are distinct; block row i only names blocks from 4 * (i // 4) - 4 to 4 * (i // 4) + 7. `h_cols`: same law as z_cols, drawn apart. `z_count`: block row 0 uses all 4 slots. `h_count`: block row 0 uses all 4 slots.
All inputs are finite; a program needn't handle non-finite values.
Results may differ from the reference program's by a relative error of at most 0.000098.
Values sent between devices are 32-bit elements; how exact they have to be, the bound alone decides.
A program may use at most 64 MiB of HBM per device.

```python
import jax
import jax.numpy as jnp
from jax import lax

BLK = 256
P_SIZE = 64
R = 4
HB = 4
KS = 4
NB = 32
WB = 12


def band_pattern(key):
    rowids = jnp.arange(NB, dtype=jnp.int32)
    lower = rowids // R * R - HB
    offsets = jnp.arange(WB, dtype=jnp.int32)
    global_cols = lower[:, None] + offsets[None, :]
    valid = (global_cols >= 0) & (global_cols < NB)
    score = jax.random.randint(key, (NB, WB), 0, 4096, dtype=jnp.int32) * WB + offsets[None, :]
    score = score + jnp.where(valid, 0, 8192 * WB)
    order = jnp.argsort(score, axis=1, stable=True)[:, :KS]
    return jnp.take_along_axis(global_cols, order, axis=1).astype(jnp.int32)


def slot_counts(key):
    counts = jax.random.randint(key, (NB,), KS // 4, KS + 1, dtype=jnp.int32)
    return jnp.where(jnp.arange(NB) == 0, KS, counts).astype(jnp.int32)


def draw_z_cols(key, part):
    return band_pattern(jax.random.fold_in(key, 11))


def draw_h_cols(key, part):
    return band_pattern(jax.random.fold_in(key, 23))


def draw_z_count(key, part):
    return slot_counts(jax.random.fold_in(key, 37))


def draw_h_count(key, part):
    return slot_counts(jax.random.fold_in(key, 41))


def steps_of(stream_key, dims, pieces, least, high):
    loudness = 1.0
    for position, blocks in pieces:
        heights = jax.random.uniform(jax.random.fold_in(jax.random.fold_in(stream_key, 6), position), (blocks,), jnp.float32, least / len(pieces), high / len(pieces))
        loudness = loudness * jnp.repeat(jnp.exp(heights), dims[position] // blocks).reshape((-1,) + (1,) * (len(dims) - 1 - position))
    return loudness


def normal_values(rng, extent, deviation, bound, cuts=(), kind=jnp.bfloat16):
    factor_of = steps_of(rng, extent, cuts, -0.22, 0.18) if cuts else 1.0
    result = jax.random.normal(rng, extent, jnp.float32) * deviation * factor_of
    return jnp.minimum(jnp.maximum(result, -bound), bound).astype(kind)


def setup_inputs(seed: int = 0) -> dict:
    splits = jax.random.split(jax.random.key(seed), 8)
    return {
        "z_blocks": normal_values(splits[0], (NB, KS, BLK, BLK), (KS * BLK) ** -0.5, 0.1875, ((0, 8), (1, 4)), jnp.float32),
        "z_cols": draw_z_cols(jax.random.fold_in(splits[7], 71), 0),
        "z_count": draw_z_count(jax.random.fold_in(splits[7], 71), 0),
        "h_blocks": normal_values(splits[3], (NB, KS, BLK, BLK), (KS * BLK) ** -0.5, 0.1875, ((0, 8), (1, 4)), jnp.float32),
        "h_cols": draw_h_cols(jax.random.fold_in(splits[7], 71), 0),
        "h_count": draw_h_count(jax.random.fold_in(splits[7], 71), 0),
        "panel": normal_values(splits[6], (NB, BLK, P_SIZE), 1.0, 6.0, ((0, 8),), jnp.float32),
    }


def used_mask(count):
    return (jnp.arange(KS)[None, :] < count[:, None]).astype(jnp.float32)


def apply_rows(blocks, cols, count, field):
    picked = field[cols] * used_mask(count)[:, :, None, None]
    return jnp.einsum('ikpq,ikqn->ipn', blocks, picked, precision=lax.Precision.HIGHEST)


def reference(z_blocks, z_cols, z_count, h_blocks, h_cols, h_count, panel):
    mid = apply_rows(z_blocks, z_cols, z_count, panel)
    side = apply_rows(h_blocks, h_cols, h_count, mid)
    terms = jnp.einsum('ikqp,iqn->ikpn', z_blocks, side, precision=lax.Precision.HIGHEST)
    terms = terms * used_mask(z_count)[:, :, None, None]
    flat = terms.reshape(NB * KS, BLK, P_SIZE)
    return jax.ops.segment_sum(flat, z_cols.reshape(-1), num_segments=NB)
```

```python
import functools

import jax
import jax.numpy as jnp
from jax import lax
from jax.experimental import pallas as pl
from jax.experimental.pallas import tpu as pltpu
from jax.sharding import PartitionSpec as P

MESH = pl.DeviceIdType.MESH
BF = jnp.bfloat16
F32 = jnp.float32


def split(x):
    hi = x.astype(BF)
    return hi, (x - hi.astype(F32)).astype(BF)


def kernel(nr, nc, own, blk, width,
           zc, zn, hc, hn, z_hbm, h_hbm, p_hbm, out,
           pan, zf, hf, zhi, zlo, thi, tlo, hhi, hlo,
           codes, codes_all, idx,
           xwin, xsend, xpick, mpart, mrecv, mwin, msend, mpick,
           spart, srecv, side, term, trecv, acc, below, above,
           local_sem, idx_sem, peer_send, peer_recv, row_send, row_recv):
    r, c = lax.axis_index("rows"), lax.axis_index("cols")
    sh = blk // nc
    np_ = own // 2
    lanes = 2 * width
    has_low, has_high = r > 0, r < nr - 1
    mine = pl.ds(pl.multiple_of(c * sh, sh), sh)

    def peer(d):
        return lax.rem(c + d, nc)

    def rows_of(q):
        return pl.ds(pl.multiple_of(q * sh, sh), sh)

    load_p = pltpu.make_async_copy(p_hbm.at[:, mine, :], pan, local_sem.at[0])
    load_z = pltpu.make_async_copy(z_hbm.at[:, 0], zf, local_sem.at[1])
    load_h = pltpu.make_async_copy(h_hbm.at[:, 0], hf, local_sem.at[2])
    load_p.start()
    load_z.start()
    load_h.start()

    barrier = pltpu.get_barrier_semaphore()
    for d in range(1, nc):
        pl.semaphore_signal(barrier, inc=1, device_id=(r, peer(d)), device_id_type=MESH)

    @pl.when(has_low)
    def _():
        pl.semaphore_signal(barrier, inc=1, device_id=(r - 1, c), device_id_type=MESH)

    @pl.when(has_high)
    def _():
        pl.semaphore_signal(barrier, inc=1, device_id=(r + 1, c), device_id_type=MESH)

    lane = lax.broadcasted_iota(jnp.int32, (1, lanes), 1)
    left = lane < width
    code_row = lax.broadcasted_iota(jnp.int32, (8, 128), 0)
    start = r * own - own
    code = jnp.zeros((8, 128), jnp.int32) - 1
    for a in range(own):
        zo = jnp.where(c < zn[a], zc[a, 0] - start, -1)
        ho = jnp.where(c < hn[a], hc[a, 0] - start, -1)
        code = jnp.where(code_row == a, zo, code)
        code = jnp.where(code_row == own + a, ho, code)
    codes[...] = code

    load_p.wait()
    for j in range(np_):
        xwin[np_ + j] = jnp.concatenate([pan[2 * j], pan[2 * j + 1]], axis=1)

    pl.semaphore_wait(barrier, nc - 1 + has_low.astype(jnp.int32) + has_high.astype(jnp.int32))

    def exchange(k, low_src, high_src, low_dst, high_dst):
        down = pltpu.make_async_remote_copy(
            low_src, high_dst, row_send.at[k, 0], row_recv.at[k, 0],
            device_id=(r - 1, c), device_id_type=MESH)
        up = pltpu.make_async_remote_copy(
            high_src, low_dst, row_send.at[k, 1], row_recv.at[k, 1],
            device_id=(r + 1, c), device_id_type=MESH)

        @pl.when(has_low)
        def _():
            down.start()

        @pl.when(has_high)
        def _():
            up.start()

        def arrive():
            @pl.when(has_low)
            def _():
                up.wait_recv()
                down.wait_send()

            @pl.when(has_high)
            def _():
                down.wait_recv()
                up.wait_send()
        return arrive

    def to_peers(k, src_of, dst_of):
        copies = []
        for d in range(1, nc):
            copies.append(pltpu.make_async_remote_copy(
                src_of(d), dst_of(d), peer_send.at[k, d - 1], peer_recv.at[k, d - 1],
                device_id=(r, peer(d)), device_id_type=MESH))
            copies[-1].start()

        def arrive():
            for copy in copies:
                copy.wait_recv()

        def sent():
            for copy in copies:
                copy.wait_send()
        return arrive, sent

    got0 = exchange(0, xwin.at[pl.ds(np_, np_)], xwin.at[pl.ds(np_, np_)],
                    xwin.at[pl.ds(0, np_)], xwin.at[pl.ds(2 * np_, np_)])
    got_codes, sent_codes = to_peers(0, lambda d: codes, lambda d: codes_all.at[d])
    codes_all[0] = code

    for win in (xwin, mwin):
        @pl.when(r == 0)
        def _():
            win[pl.ds(0, np_)] = jnp.zeros((np_, sh, lanes), F32)

        @pl.when(r == nr - 1)
        def _():
            win[pl.ds(2 * np_, np_)] = jnp.zeros((np_, sh, lanes), F32)

    load_z.wait()
    for a in range(own):
        z = zf[a]
        zhi[a], zlo[a] = split(z)
    got_codes()
    to_smem = pltpu.make_async_copy(codes_all, idx, idx_sem)
    to_smem.start()
    to_smem.wait()

    def code_of(d, row):
        return idx[(nc - d) % nc, row, 0]

    def pick(win, d, base, send, own_dst):
        for j in range(np_):
            halves = []
            for h in range(2):
                off = code_of(d, base + 2 * j + h)
                at = jnp.maximum(off, 0)
                pair = win[at // 2]
                swapped = pltpu.roll(pair, width, 1)
                use = jnp.where(at % 2 == h, pair, swapped)
                halves.append(jnp.where(off >= 0, use, 0.0))
            both = jnp.where(left, halves[0], halves[1])
            if d == 0:
                own_dst[j, mine, :] = both
            else:
                send[d - 1, j] = both

    def apply(hi_ref, lo_ref, src, dst):
        for j in range(np_):
            hi, lo = split(src[j])
            cat = jnp.concatenate([hi, lo], axis=1)
            res = []
            for a in (2 * j, 2 * j + 1):
                wide = jnp.dot(hi_ref[a], cat, preferred_element_type=F32)
                slim = jnp.dot(lo_ref[a], hi, preferred_element_type=F32)
                res.append(wide[:, :lanes] + (wide[:, lanes:] + slim))
            dst[j] = jnp.where(left, res[0], res[1])

    def pick_all(k, win, base, send, dst):
        copies = []
        for d in list(range(1, nc)) + [0]:
            pick(win, d, base, send, dst)
            if d:
                copies.append(pltpu.make_async_remote_copy(
                    send.at[d - 1], dst.at[:, mine, :],
                    peer_send.at[k, d - 1], peer_recv.at[k, d - 1],
                    device_id=(r, peer(d)), device_id_type=MESH))
                copies[-1].start()
        return copies

    def recv_all(copies, dst, k):
        for d in range(1, nc):
            q = lax.rem(c + nc - d, nc)
            pltpu.make_async_remote_copy(
                dst.at[:, rows_of(q), :], dst.at[:, rows_of(q), :],
                peer_send.at[k, d - 1], peer_recv.at[k, d - 1],
                device_id=(r, peer(d)), device_id_type=MESH).wait_recv()

    got0()
    copies_x = pick_all(1, xwin, 0, xsend, xpick)
    load_h.wait()
    for a in range(own):
        hhi[a], hlo[a] = split(hf[a])
    recv_all(copies_x, xpick, 1)
    apply(zhi, zlo, xpick, mpart)

    def reduce(k, part, recv, store):
        arrive, sent = to_peers(k, lambda d: part.at[:, rows_of(peer(d)), :],
                                lambda d: recv.at[d - 1])
        if k == 2:
            for a in range(own):
                thi[a], tlo[a] = split(zf[a].T)
        arrive()
        for j in range(np_):
            total = part[j, mine, :]
            for d in range(1, nc):
                total = total + recv[d - 1, j]
            store(j, total)
        return sent

    def store_mid(j, v):
        mwin[np_ + j] = v

    sent_m = reduce(2, mpart, mrecv, store_mid)
    got1 = exchange(1, mwin.at[pl.ds(np_, np_)], mwin.at[pl.ds(np_, np_)],
                    mwin.at[pl.ds(0, np_)], mwin.at[pl.ds(2 * np_, np_)])
    got1()
    copies_m = pick_all(3, mwin, own, msend, mpick)
    recv_all(copies_m, mpick, 3)
    apply(hhi, hlo, mpick, spart)

    def store_side(j, v):
        side[j, mine, :] = v

    sent_s = reduce(4, spart, srecv, store_side)
    copies_s = []
    for d in range(1, nc):
        copies_s.append(pltpu.make_async_remote_copy(
            side.at[:, mine, :], side.at[:, mine, :],
            peer_send.at[5, d - 1], peer_recv.at[5, d - 1],
            device_id=(r, peer(d)), device_id_type=MESH))
        copies_s[-1].start()
    recv_all(copies_s, side, 5)
    apply(thi, tlo, side, term)

    arrive_t, sent_t = to_peers(6, lambda d: term.at[:, rows_of(peer(d)), :],
                                lambda d: trecv.at[d - 1])
    sums = [jnp.zeros((sh, lanes), F32) for _ in range(3 * np_)]
    half = jnp.where(left, 0, 1)
    for d in range(nc):
        if d == 1:
            arrive_t()
        for j in range(np_):
            t = term[j, mine, :] if d == 0 else trecv[d - 1, j]
            swapped = pltpu.roll(t, width, 1)
            for h in range(2):
                dup = jnp.where(left, t, swapped) if h == 0 else jnp.where(left, swapped, t)
                off = idx[d, 2 * j + h, 0]
                for p in range(3 * np_):
                    sums[p] = sums[p] + jnp.where(half == off - 2 * p, dup, 0.0)
    for p in range(3 * np_):
        acc[p] = sums[p]
    got2 = exchange(2, acc.at[pl.ds(0, np_)], acc.at[pl.ds(2 * np_, np_)], below, above)

    @pl.when(r == 0)
    def _():
        below[...] = jnp.zeros(below.shape, F32)

    @pl.when(r == nr - 1)
    def _():
        above[...] = jnp.zeros(above.shape, F32)

    sent_codes()
    for copy in copies_x + copies_m + copies_s:
        copy.wait_send()
    sent_m()
    sent_s()
    sent_t()
    got2()
    for j in range(np_):
        total = acc[np_ + j] + below[j] + above[j]
        out[2 * j] = total[:, :width]
        out[2 * j + 1] = total[:, width:]


def local(nr, nc, z_blocks, z_cols, z_count, h_blocks, h_cols, h_count, panel):
    own, blk, width = panel.shape
    sh, np_, lanes = blk // nc, own // 2, 2 * width
    f = lambda *s: pltpu.VMEM(s, F32)
    b = lambda *s: pltpu.VMEM(s, BF)
    dma = pltpu.SemaphoreType.DMA
    smem = pl.BlockSpec(memory_space=pltpu.SMEM)
    hbm = pl.BlockSpec(memory_space=pl.ANY)
    full = (np_, blk, lanes)
    peers = (nc - 1, np_, sh, lanes)
    return pl.pallas_call(
        functools.partial(kernel, nr, nc, own, blk, width),
        out_shape=jax.ShapeDtypeStruct((own, sh, width), F32),
        in_specs=[smem] * 4 + [hbm] * 3,
        out_specs=pl.BlockSpec(memory_space=pltpu.VMEM),
        scratch_shapes=[
            f(own, sh, width), f(own, blk, blk), f(own, blk, blk),
            b(own, blk, blk), b(own, blk, blk), b(own, blk, blk),
            b(own, blk, blk), b(own, blk, blk), b(own, blk, blk),
            pltpu.VMEM((8, 128), jnp.int32), pltpu.VMEM((nc, 8, 128), jnp.int32),
            pltpu.SMEM((nc, 8, 128), jnp.int32),
            f(3 * np_, sh, lanes), f(*peers), f(*full), f(*full), f(*peers),
            f(3 * np_, sh, lanes), f(*peers), f(*full),
            f(*full), f(*peers), f(*full), f(*full), f(*peers),
            f(3 * np_, sh, lanes), f(np_, sh, lanes), f(np_, sh, lanes),
            dma((3,)), dma, dma((7, nc - 1)), dma((7, nc - 1)), dma((3, 2)), dma((3, 2)),
        ],
        compiler_params=pltpu.CompilerParams(
            collective_id=0, has_side_effects=True, vmem_limit_bytes=32 * 1024 * 1024),
    )(z_cols, z_count, h_cols, h_count, z_blocks, h_blocks, panel)


def solution(mesh):
    return jax.shard_map(
        functools.partial(local, mesh.shape["rows"], mesh.shape["cols"]),
        mesh=mesh,
        in_specs=(
            P("rows", "cols", None, None),
            P("rows", "cols"),
            P("rows"),
            P("rows", "cols", None, None),
            P("rows", "cols"),
            P("rows"),
            P("rows", None, None),
        ),
        out_specs=P("rows", "cols", None),
        check_vma=False,
    )
```

```python
import functools

import jax
import jax.numpy as jnp
from jax import lax
from jax.experimental import pallas as pl
from jax.experimental.pallas import tpu as pltpu
from jax.sharding import PartitionSpec as P

MESH = pl.DeviceIdType.MESH
BF = jnp.bfloat16
F32 = jnp.float32


def split(x):
    hi = x.astype(BF)
    return hi, (x - hi.astype(F32)).astype(BF)


def kernel(nr, nc, own, blk, width, w,
           zc, zn, hc, hn, z_hbm, h_hbm, p_hbm, out,
           pan, zf, hf, zhi, zlo, thi, tlo, hhi, hlo,
           codes, codes_all, idx, xfull, xwin, xsend, xpick, mpart, mrecv, mwin, msend, mpick,
           spart, srecv, side, term, trecv, acc, rims,
           local_sem, idx_sem, code_send, code_recv,
           peer_send, peer_recv, row_send, row_recv):
    r, c = lax.axis_index("rows"), lax.axis_index("cols")
    sh = blk // nc
    lanes = own * w
    has_low, has_high = r > 0, r < nr - 1

    def peer(d):
        return lax.rem(c + d, nc)

    def rows_of(q):
        return pl.ds(pl.multiple_of(q * sh, sh), sh)

    mine = rows_of(c)
    load_p = pltpu.make_async_copy(p_hbm, pan, local_sem.at[0])
    load_z = pltpu.make_async_copy(z_hbm.at[:, 0], zf, local_sem.at[1])
    load_h = pltpu.make_async_copy(h_hbm.at[:, 0], hf, local_sem.at[2])
    load_p.start()
    load_z.start()
    load_h.start()

    barrier = pltpu.get_barrier_semaphore()
    for d in range(1, nc):
        pl.semaphore_signal(barrier, inc=1, device_id=(r, peer(d)), device_id_type=MESH)

    @pl.when(has_low)
    def _():
        pl.semaphore_signal(barrier, inc=1, device_id=(r - 1, c), device_id_type=MESH)

    @pl.when(has_high)
    def _():
        pl.semaphore_signal(barrier, inc=1, device_id=(r + 1, c), device_id_type=MESH)

    part_of_lane = lax.broadcasted_iota(jnp.int32, (1, lanes), 1) // w
    code_row = lax.broadcasted_iota(jnp.int32, (8, 128), 0)
    start = r * own - own
    code = jnp.zeros((8, 128), jnp.int32) - 1
    for a in range(own):
        zo = jnp.where(c < zn[a], zc[a] - start, -1)
        ho = jnp.where(c < hn[a], hc[a] - start, -1)
        code = jnp.where(code_row == a, zo, code)
        code = jnp.where(code_row == own + a, ho, code)
    codes[...] = code
    codes_all[0] = code

    chains = width // w
    load_p.wait()
    for g in range(chains):
        flat = jnp.concatenate([pan[a, g * w:(g + 1) * w, :] for a in range(own)], axis=0)
        xfull[g] = flat.T
        xwin[g, 1] = xfull[g, mine, :]

    for win in (xwin, mwin):
        @pl.when(r == 0)
        def _():
            win[:, 0] = jnp.zeros((chains, sh, lanes), F32)

        @pl.when(r == nr - 1)
        def _():
            win[:, 2] = jnp.zeros((chains, sh, lanes), F32)

    @pl.when(r == 0)
    def _():
        rims[:, 0] = jnp.zeros((chains, sh, lanes), F32)

    @pl.when(r == nr - 1)
    def _():
        rims[:, 1] = jnp.zeros((chains, sh, lanes), F32)

    pl.semaphore_wait(barrier, nc - 1 + has_low.astype(jnp.int32) + has_high.astype(jnp.int32))

    unsent = []

    def exchange(g, k, to_low, to_high, from_low, from_high):
        down = pltpu.make_async_remote_copy(
            to_low, from_high, row_send.at[g, k, 0], row_recv.at[g, k, 0],
            device_id=(r - 1, c), device_id_type=MESH)
        up = pltpu.make_async_remote_copy(
            to_high, from_low, row_send.at[g, k, 1], row_recv.at[g, k, 1],
            device_id=(r + 1, c), device_id_type=MESH)

        @pl.when(has_low)
        def _():
            down.start()

        @pl.when(has_high)
        def _():
            up.start()

        def arrive():
            @pl.when(has_low)
            def _():
                up.wait_recv()

            @pl.when(has_high)
            def _():
                down.wait_recv()

        def sent():
            @pl.when(has_low)
            def _():
                down.wait_send()

            @pl.when(has_high)
            def _():
                up.wait_send()
        unsent.append(sent)
        return arrive

    def send(g, k, d, src, dst):
        copy = pltpu.make_async_remote_copy(
            src, dst, peer_send.at[g, k, d - 1], peer_recv.at[g, k, d - 1],
            device_id=(r, peer(d)), device_id_type=MESH)
        copy.start()
        unsent.append(copy.wait_send)
        return copy

    def arrive_rows(g, k, dst):
        for d in range(1, nc):
            here = dst.at[rows_of(lax.rem(c + nc - d, nc)), :]
            pltpu.make_async_remote_copy(
                here, here, peer_send.at[g, k, d - 1], peer_recv.at[g, k, d - 1],
                device_id=(r, peer(d)), device_id_type=MESH).wait_recv()

    def everywhere(x):
        step = lanes // 2
        while step >= w:
            x = x + pltpu.roll(x, step, 1)
            step //= 2
        return x

    def picks(g, k, win, base, buf, dst):
        for d in list(range(1, nc)) + [0]:
            both = jnp.zeros((sh, lanes), F32)
            for h in range(own):
                off = idx[(nc - d) % nc, base + h, 0]
                one = jnp.zeros((sh, lanes), F32)
                for p in range(3):
                    one = jnp.where(part_of_lane == off - own * p, win[p], one)
                both = jnp.where(part_of_lane == h, everywhere(one), both)
            if d:
                buf[d - 1] = both
                send(g, k, d, buf.at[d - 1], dst.at[mine, :])
            else:
                dst[mine, :] = both

    def apply(hi_ref, lo_ref, src, dst):
        hi, lo = split(src[...])
        cat = jnp.concatenate([hi, lo], axis=1)
        res = None
        for a in range(own):
            wide = jnp.dot(hi_ref[a], cat, preferred_element_type=F32)
            slim = jnp.dot(lo_ref[a], hi, preferred_element_type=F32)
            one = wide[:, :lanes] + (wide[:, lanes:] + slim)
            res = one if a == 0 else jnp.where(part_of_lane == a, one, res)
        dst[...] = res

    def scatter(g, k, part, recv):
        return [send(g, k, d, part.at[rows_of(peer(d)), :], recv.at[d - 1])
                for d in range(1, nc)]

    def total(part, recv, copies):
        value = part[mine, :]
        for d in range(1, nc):
            copies[d - 1].wait_recv()
            value = value + recv[d - 1]
        return value

    def chain(g):
        xw, mw = xwin.at[g], mwin.at[g]
        got = exchange(g, 0, xw.at[1], xw.at[1], xw.at[0], xw.at[2])
        yield
        got()
        picks(g, 0, xw, 0, xsend.at[g], xpick.at[g])
        yield
        arrive_rows(g, 0, xpick.at[g])
        apply(zhi, zlo, xpick.at[g], mpart.at[g])
        copies = scatter(g, 1, mpart.at[g], mrecv.at[g])
        yield
        mw[1] = total(mpart.at[g], mrecv.at[g], copies)
        got = exchange(g, 1, mw.at[1], mw.at[1], mw.at[0], mw.at[2])
        yield
        got()
        picks(g, 2, mw, own, msend.at[g], mpick.at[g])
        yield
        arrive_rows(g, 2, mpick.at[g])
        apply(hhi, hlo, mpick.at[g], spart.at[g])
        copies = scatter(g, 3, spart.at[g], srecv.at[g])
        yield
        whole = side.at[g]
        whole[mine, :] = total(spart.at[g], srecv.at[g], copies)
        for d in range(1, nc):
            send(g, 4, d, whole.at[mine, :], whole.at[mine, :])
        yield
        arrive_rows(g, 4, whole)
        apply(thi, tlo, whole, term.at[g])
        copies = scatter(g, 5, term.at[g], trecv.at[g])
        yield
        sums = [jnp.zeros((sh, lanes), F32) for _ in range(3)]
        for d in range(nc):
            if d:
                copies[d - 1].wait_recv()
            t = trecv[g, d - 1] if d else term[g, mine, :]
            for a in range(own):
                off = idx[d, a, 0]
                dup = everywhere(jnp.where(part_of_lane == a, t, 0.0))
                for p in range(3):
                    sums[p] = sums[p] + jnp.where(part_of_lane == off - own * p, dup, 0.0)
        for p in range(3):
            acc[g, p] = sums[p]
        got = exchange(g, 2, acc.at[g, 0], acc.at[g, 2], rims.at[g, 0], rims.at[g, 1])
        yield
        got()

    def advance():
        for one in running:
            next(one, None)

    running = [chain(g) for g in range(chains)]
    code_copies = []
    for d in range(1, nc):
        code_copies.append(pltpu.make_async_remote_copy(
            codes, codes_all.at[d], code_send.at[d - 1], code_recv.at[d - 1],
            device_id=(r, peer(d)), device_id_type=MESH))
        code_copies[-1].start()
    advance()
    load_z.wait()
    for a in range(own):
        zhi[a], zlo[a] = split(zf[a])
    for copy in code_copies:
        copy.wait_recv()
    to_smem = pltpu.make_async_copy(codes_all, idx, idx_sem)
    to_smem.start()
    to_smem.wait()
    advance()
    load_h.wait()
    for a in range(own):
        hhi[a], hlo[a] = split(hf[a])
    advance()
    for a in range(own):
        thi[a], tlo[a] = split(zf[a].T)
    for _ in range(6):
        advance()
    for copy in code_copies:
        copy.wait_send()
    for sent in unsent:
        sent()
    advance()
    sums = [acc[g, 1] + rims[g, 0] + rims[g, 1] for g in range(chains)]
    for a in range(own):
        out[a] = jnp.concatenate([s[:, a * w:(a + 1) * w] for s in sums], axis=1)


def local(nr, nc, z_blocks, z_cols, z_count, h_blocks, h_cols, h_count, panel):
    own, blk, width = panel.shape
    w = min(width, 128 // own)
    g, sh, lanes = width // w, blk // nc, own * w
    f = lambda *s: pltpu.VMEM(s, F32)
    halves = pltpu.VMEM((own, blk, blk), BF)
    dma = pltpu.SemaphoreType.DMA
    smem = pl.BlockSpec(memory_space=pltpu.SMEM)
    hbm = pl.BlockSpec(memory_space=pltpu.HBM)
    full, peers, window = f(g, blk, lanes), f(g, nc - 1, sh, lanes), f(g, 3, sh, lanes)
    return pl.pallas_call(
        functools.partial(kernel, nr, nc, own, blk, width, w),
        out_shape=jax.ShapeDtypeStruct((own, sh, width), F32),
        in_specs=[smem] * 4 + [hbm] * 3,
        out_specs=pl.BlockSpec(memory_space=pltpu.VMEM),
        scratch_shapes=[
            f(own, width, blk), f(own, blk, blk), f(own, blk, blk),
        ] + [halves] * 6 + [
            pltpu.VMEM((8, 128), jnp.int32), pltpu.VMEM((nc, 8, 128), jnp.int32),
            pltpu.SMEM((nc, 8, 128), jnp.int32),
            full, window, peers, full, full, peers, window, peers, full,
            full, peers, full, full, peers, window, f(g, 2, sh, lanes),
            dma((3,)), dma, dma((nc - 1,)), dma((nc - 1,)),
            dma((g, 6, nc - 1)), dma((g, 6, nc - 1)), dma((g, 3, 2)), dma((g, 3, 2)),
        ],
        compiler_params=pltpu.CompilerParams(
            collective_id=0, has_side_effects=True, vmem_limit_bytes=60 * 1024 * 1024),
    )(z_cols.reshape(-1), z_count, h_cols.reshape(-1), h_count, z_blocks, h_blocks,
      jnp.swapaxes(panel, 1, 2))


def solution(mesh):
    return jax.shard_map(
        functools.partial(local, mesh.shape["rows"], mesh.shape["cols"]),
        mesh=mesh,
        in_specs=(
            P("rows", "cols", None, None),
            P("rows", "cols"),
            P("rows"),
            P("rows", "cols", None, None),
            P("rows", "cols"),
            P("rows"),
            P("rows", None, None),
        ),
        out_specs=P("rows", "cols", None),
        check_vma=False,
    )
```

```python
import functools

import jax
import jax.numpy as jnp
from jax import lax
from jax.experimental import pallas as pl
from jax.experimental.pallas import tpu as pltpu
from jax.sharding import PartitionSpec as P

MESH = pl.DeviceIdType.MESH
BF = jnp.bfloat16
F32 = jnp.float32


def split(x):
    hi = x.astype(BF)
    return hi, (x - hi.astype(F32)).astype(BF)


def kernel(nr, nc, own, blk, width, w,
           zc, zn, hc, hn, z_hbm, h_hbm, p_hbm, out,
           pan, zf, hf, zhi, zlo, thi, tlo, hhi, hlo,
           codes, codes_all, idx, xfull, xwin, xsend, xpick, mpart, mrecv, mwin, msend, mpick,
           spart, srecv, side, term, trecv, acc, rims, mpair, spair, mhalf, shalf,
           local_sem, idx_sem, code_send, code_recv,
           peer_send, peer_recv, row_send, row_recv):
    r, c = lax.axis_index("rows"), lax.axis_index("cols")
    sh = blk // nc
    lanes = own * w
    nx = nc // 2
    x, core = c // 2, lax.rem(c, 2)
    has_low, has_high = r > 0, r < nr - 1

    def peer(d):
        return lax.rem(c + d, nc)

    def rows_of(q):
        return pl.ds(pl.multiple_of(q * sh, sh), sh)

    mine = rows_of(c)
    load_p = pltpu.make_async_copy(p_hbm, pan, local_sem.at[0])
    load_z = pltpu.make_async_copy(z_hbm.at[:, 0], zf, local_sem.at[1])
    load_h = pltpu.make_async_copy(h_hbm.at[:, 0], hf, local_sem.at[2])
    load_p.start()
    load_z.start()
    load_h.start()

    barrier = pltpu.get_barrier_semaphore()
    for d in range(1, nc):
        pl.semaphore_signal(barrier, inc=1, device_id=(r, peer(d)), device_id_type=MESH)

    @pl.when(has_low)
    def _():
        pl.semaphore_signal(barrier, inc=1, device_id=(r - 1, c), device_id_type=MESH)

    @pl.when(has_high)
    def _():
        pl.semaphore_signal(barrier, inc=1, device_id=(r + 1, c), device_id_type=MESH)

    part_of_lane = lax.broadcasted_iota(jnp.int32, (1, lanes), 1) // w
    code_row = lax.broadcasted_iota(jnp.int32, (8, 128), 0)
    start = r * own - own
    code = jnp.zeros((8, 128), jnp.int32) - 1
    for a in range(own):
        zo = jnp.where(c < zn[a], zc[a] - start, -1)
        ho = jnp.where(c < hn[a], hc[a] - start, -1)
        code = jnp.where(code_row == a, zo, code)
        code = jnp.where(code_row == own + a, ho, code)
    codes[...] = code
    codes_all[0] = code

    chains = width // w
    load_p.wait()
    for g in range(chains):
        flat = jnp.concatenate([pan[a, g * w:(g + 1) * w, :] for a in range(own)], axis=0)
        xfull[g] = flat.T
        xwin[g, 1] = xfull[g, mine, :]

    for win in (xwin, mwin):
        @pl.when(r == 0)
        def _():
            win[:, 0] = jnp.zeros((chains, sh, lanes), F32)

        @pl.when(r == nr - 1)
        def _():
            win[:, 2] = jnp.zeros((chains, sh, lanes), F32)

    @pl.when(r == 0)
    def _():
        rims[:, 0] = jnp.zeros((chains, sh, lanes), F32)

    @pl.when(r == nr - 1)
    def _():
        rims[:, 1] = jnp.zeros((chains, sh, lanes), F32)

    pl.semaphore_wait(barrier, nc - 1 + has_low.astype(jnp.int32) + has_high.astype(jnp.int32))

    unsent = []

    def exchange(g, k, to_low, to_high, from_low, from_high):
        down = pltpu.make_async_remote_copy(
            to_low, from_high, row_send.at[g, k, 0], row_recv.at[g, k, 0],
            device_id=(r - 1, c), device_id_type=MESH)
        up = pltpu.make_async_remote_copy(
            to_high, from_low, row_send.at[g, k, 1], row_recv.at[g, k, 1],
            device_id=(r + 1, c), device_id_type=MESH)

        @pl.when(has_low)
        def _():
            down.start()

        @pl.when(has_high)
        def _():
            up.start()

        def arrive():
            @pl.when(has_low)
            def _():
                up.wait_recv()

            @pl.when(has_high)
            def _():
                down.wait_recv()

        def sent():
            @pl.when(has_low)
            def _():
                down.wait_send()

            @pl.when(has_high)
            def _():
                up.wait_send()
        unsent.append(sent)
        return arrive

    def send(g, k, d, src, dst, target=None):
        copy = pltpu.make_async_remote_copy(
            src, dst, peer_send.at[g, k, d - 1], peer_recv.at[g, k, d - 1],
            device_id=(r, peer(d) if target is None else target), device_id_type=MESH)
        copy.start()
        unsent.append(copy.wait_send)
        return copy

    def arrive_rows(g, k, dst):
        for d in range(1, nc):
            here = dst.at[rows_of(lax.rem(c + nc - d, nc)), :]
            pltpu.make_async_remote_copy(
                here, here, peer_send.at[g, k, d - 1], peer_recv.at[g, k, d - 1],
                device_id=(r, peer(d)), device_id_type=MESH).wait_recv()

    def everywhere(x):
        step = lanes // 2
        while step >= w:
            x = x + pltpu.roll(x, step, 1)
            step //= 2
        return x

    def picks(g, k, win, base, buf, dst):
        for d in list(range(1, nc)) + [0]:
            both = jnp.zeros((sh, lanes), F32)
            for h in range(own):
                off = idx[(nc - d) % nc, base + h, 0]
                one = jnp.zeros((sh, lanes), F32)
                for p in range(3):
                    one = jnp.where(part_of_lane == off - own * p, win[p], one)
                both = jnp.where(part_of_lane == h, everywhere(one), both)
            if d:
                buf[d - 1] = both
                send(g, k, d, buf.at[d - 1], dst.at[mine, :])
            else:
                dst[mine, :] = both

    def apply(hi_ref, lo_ref, src, dst):
        hi, lo = split(src[...].reshape(blk, lanes))
        cat = jnp.concatenate([hi, lo], axis=1)
        res = None
        for a in range(own):
            wide = jnp.dot(hi_ref[a], cat, preferred_element_type=F32)
            slim = jnp.dot(lo_ref[a], hi, preferred_element_type=F32)
            one = wide[:, :lanes] + (wide[:, lanes:] + slim)
            res = one if a == 0 else jnp.where(part_of_lane == a, one, res)
        dst[...] = res.reshape(dst.shape)

    def scatter(g, k, part, recv):
        return [send(g, k, d, part.at[rows_of(peer(d)), :], recv.at[d - 1])
                for d in range(1, nc)]

    def to_partner(g, k, part, recv):
        return send(g, k, 1, part.at[:, 1 - core], recv, c + 1 - 2 * core)

    def across(d):
        return lax.rem(x + d, nx)

    def chain(g):
        xw, mw = xwin.at[g], mwin.at[g]
        got = exchange(g, 0, xw.at[1], xw.at[1], xw.at[0], xw.at[2])
        yield
        got()
        picks(g, 0, xw, 0, xsend.at[g], xpick.at[g])
        yield
        arrive_rows(g, 0, xpick.at[g])
        apply(zhi, zlo, xpick.at[g], mpart.at[g])
        copy = to_partner(g, 1, mpart.at[g], mpair.at[g])
        yield
        copy.wait_recv()
        mhalf[g] = mpart[g, :, core] + mpair[g]
        copies = [send(g, 6, d, mhalf.at[g, across(d)], mrecv.at[g, d - 1],
                       2 * across(d) + core) for d in range(1, nx)]
        yield
        value = mhalf[g, x]
        for d in range(1, nx):
            copies[d - 1].wait_recv()
            value = value + mrecv[g, d - 1]
        mw[1] = value
        got = exchange(g, 1, mw.at[1], mw.at[1], mw.at[0], mw.at[2])
        yield
        got()
        picks(g, 2, mw, own, msend.at[g], mpick.at[g])
        yield
        arrive_rows(g, 2, mpick.at[g])
        apply(hhi, hlo, mpick.at[g], spart.at[g])
        copy = to_partner(g, 3, spart.at[g], spair.at[g])
        yield
        copy.wait_recv()
        shalf[g] = spart[g, :, core] + spair[g]
        copies = [send(g, 7, d, shalf.at[g], srecv.at[g, d - 1],
                       2 * across(d) + core) for d in range(1, nx)]
        yield
        value = shalf[g]
        for d in range(1, nx):
            copies[d - 1].wait_recv()
            value = value + srecv[g, d - 1]
        side[g, :, core] = value
        send(g, 4, 1, side.at[g, :, core], side.at[g, :, core], c + 1 - 2 * core)
        yield
        there = side.at[g, :, 1 - core]
        pltpu.make_async_remote_copy(
            there, there, peer_send.at[g, 4, 0], peer_recv.at[g, 4, 0],
            device_id=(r, c + 1 - 2 * core), device_id_type=MESH).wait_recv()
        apply(thi, tlo, side.at[g], term.at[g])
        copies = scatter(g, 5, term.at[g], trecv.at[g])
        yield
        sums = [jnp.zeros((sh, lanes), F32) for _ in range(3)]
        for d in range(nc):
            if d:
                copies[d - 1].wait_recv()
            t = trecv[g, d - 1] if d else term[g, mine, :]
            for a in range(own):
                off = idx[d, a, 0]
                dup = everywhere(jnp.where(part_of_lane == a, t, 0.0))
                for p in range(3):
                    sums[p] = sums[p] + jnp.where(part_of_lane == off - own * p, dup, 0.0)
        for p in range(3):
            acc[g, p] = sums[p]
        got = exchange(g, 2, acc.at[g, 0], acc.at[g, 2], rims.at[g, 0], rims.at[g, 1])
        yield
        got()

    def advance():
        for one in running:
            next(one, None)

    running = [chain(g) for g in range(chains)]
    code_copies = []
    for d in range(1, nc):
        code_copies.append(pltpu.make_async_remote_copy(
            codes, codes_all.at[d], code_send.at[d - 1], code_recv.at[d - 1],
            device_id=(r, peer(d)), device_id_type=MESH))
        code_copies[-1].start()
    advance()
    load_z.wait()
    for a in range(own):
        zhi[a], zlo[a] = split(zf[a])
    for copy in code_copies:
        copy.wait_recv()
    to_smem = pltpu.make_async_copy(codes_all, idx, idx_sem)
    to_smem.start()
    to_smem.wait()
    advance()
    load_h.wait()
    for a in range(own):
        hhi[a], hlo[a] = split(hf[a])
    advance()
    for a in range(own):
        thi[a], tlo[a] = split(zf[a].T)
    for _ in range(8):
        advance()
    for copy in code_copies:
        copy.wait_send()
    for sent in unsent:
        sent()
    advance()
    sums = [acc[g, 1] + rims[g, 0] + rims[g, 1] for g in range(chains)]
    for a in range(own):
        out[a] = jnp.concatenate([s[:, a * w:(a + 1) * w] for s in sums], axis=1)


def local(nr, nc, z_blocks, z_cols, z_count, h_blocks, h_cols, h_count, panel):
    own, blk, width = panel.shape
    w = min(width, 128 // own)
    g, sh, lanes = width // w, blk // nc, own * w
    f = lambda *s: pltpu.VMEM(s, F32)
    halves = pltpu.VMEM((own, blk, blk), BF)
    dma = pltpu.SemaphoreType.DMA
    smem = pl.BlockSpec(memory_space=pltpu.SMEM)
    hbm = pl.BlockSpec(memory_space=pltpu.HBM)
    nx = nc // 2
    split_full, part = f(g, nx, 2, sh, lanes), f(g, nx, sh, lanes)
    full, peers, window = f(g, blk, lanes), f(g, nc - 1, sh, lanes), f(g, 3, sh, lanes)
    return pl.pallas_call(
        functools.partial(kernel, nr, nc, own, blk, width, w),
        out_shape=jax.ShapeDtypeStruct((own, sh, width), F32),
        in_specs=[smem] * 4 + [hbm] * 3,
        out_specs=pl.BlockSpec(memory_space=pltpu.VMEM),
        scratch_shapes=[
            f(own, width, blk), f(own, blk, blk), f(own, blk, blk),
        ] + [halves] * 6 + [
            pltpu.VMEM((8, 128), jnp.int32), pltpu.VMEM((nc, 8, 128), jnp.int32),
            pltpu.SMEM((nc, 8, 128), jnp.int32),
            full, window, peers, full, split_full, f(g, nx - 1, sh, lanes), window, peers, full,
            split_full, f(g, nx - 1, nx, sh, lanes), split_full, full, peers, window,
            f(g, 2, sh, lanes), part, part, part, part,
            dma((3,)), dma, dma((nc - 1,)), dma((nc - 1,)),
            dma((g, 8, nc - 1)), dma((g, 8, nc - 1)), dma((g, 3, 2)), dma((g, 3, 2)),
        ],
        compiler_params=pltpu.CompilerParams(
            collective_id=0, has_side_effects=True, vmem_limit_bytes=60 * 1024 * 1024),
    )(z_cols.reshape(-1), z_count, h_cols.reshape(-1), h_count, z_blocks, h_blocks,
      jnp.swapaxes(panel, 1, 2))


def solution(mesh):
    return jax.shard_map(
        functools.partial(local, mesh.shape["rows"], mesh.shape["cols"]),
        mesh=mesh,
        in_specs=(
            P("rows", "cols", None, None),
            P("rows", "cols"),
            P("rows"),
            P("rows", "cols", None, None),
            P("rows", "cols"),
            P("rows"),
            P("rows", None, None),
        ),
        out_specs=P("rows", "cols", None),
        check_vma=False,
    )
```
